512 devices in a mesh: tm: 32 (over z, core), state: 16 (over y, x).
Axes of the slice: x: 4, y: 4, z: 16, core: 2. Of those that a mesh axis runs over, the one named last changes fastest.
Arguments:
- transition: bfloat16 [32, 1280, 1280], P('tm', 'state'), may hold values from -1 to 1
- covariance: bfloat16 [32, 1280, 1280], P('tm', 'state'), may hold values from -1 to 1, as said below
- information: bfloat16 [32, 1280, 1280], P('tm', 'state'), may hold values from -1 to 1, as said below
- offset_vec: float32 [32, 1280], P('tm', 'state'), may hold values from -6 to 6
- info_vec: float32 [32, 1280], P('tm', 'state'), may hold values from -6 to 6
- step_counts: int32 [32], P('tm'), may hold values from 1 to 8
- scan_level: int32 [1], replicated, may hold values from 0 to 4
Outputs:
- new_trans: bfloat16 [32, 1280, 1280], P('tm', 'state')
- new_covariance: bfloat16 [32, 1280, 1280], P('tm', 'state')
- new_offset: float32 [32, 1280], P('tm', 'state')
- new_counts: int32 [32], P('tm')
The draws below stay inside these ranges and needn't reach their ends.
Inputs may be any that keep to these rules, and one draw needn't show every extreme that they name: `scan_level`: the partner distance is 2 to this power. `covariance`: each block's matrix is symmetric and positive definite. `information`: each block's matrix is symmetric and positive definite.
All inputs are finite; a program needn't handle non-finite values.
Results may differ from the reference program's by a relative error of at most 0.008.
Values may be sent and summed in bfloat16 or wider, within the bound.
No kernel may reach another device: no remote copies, remote signals or barrier semaphores. Data moves between devices by JAX's collectives and lax.ppermute only.
A program may use at most 64 MiB of HBM per device.

```python
import math
import jax
import jax.numpy as jnp
from jax import lax

N = 1280
MOST_STEPS = 8
BLOCKS = 32
LEVELS = 5


def symmetric_draw(key, overall):
    spread_off = 1.0 / math.sqrt(N)
    rough = jax.random.uniform(key, (BLOCKS, N, N), jnp.float32, -spread_off, spread_off)
    paired = 0.5 * (rough + jnp.swapaxes(rough, 1, 2))
    diagonal = jax.random.uniform(jax.random.fold_in(key, 1), (BLOCKS, N, 1), jnp.float32, 1.0, 2.0)
    identity = jnp.eye(N, dtype=jnp.float32)
    return (overall * (paired * (1.0 - identity) + identity * diagonal)).astype(jnp.bfloat16)


def draw_covariance(key, part):
    key = jax.random.fold_in(key, 5)
    return symmetric_draw(key, 0.5)


def draw_information(key, part):
    key = jax.random.fold_in(key, 7)
    return symmetric_draw(key, 0.5)


def draw_transition(key, part):
    key = jax.random.fold_in(key, 11)
    spread_off = 0.85 / math.sqrt(N)
    rough = jax.random.uniform(key, (BLOCKS, N, N), jnp.float32, -spread_off, spread_off)
    diagonal = jax.random.uniform(jax.random.fold_in(key, 1), (BLOCKS, N, 1), jnp.float32, 0.5, 0.9)
    identity = jnp.eye(N, dtype=jnp.float32)
    return (rough * (1.0 - identity) + identity * diagonal).astype(jnp.bfloat16)


def plant(array, stream_key, smallest, largest):
    longest = array.shape.index(max(array.shape))
    spots = []
    for shift in (0, 1):
        where = [jax.random.randint(jax.random.fold_in(stream_key, axis), (), 0, length) for axis, length in enumerate(array.shape)]
        where[longest] = (where[longest] + shift) % array.shape[longest]
        spots.append(tuple(where))
    return array.at[spots[0]].set(smallest).at[spots[1]].set(largest)


def steps_of(key, dims, split, least, top_value):
    factor_of, own = 1.0, jax.random.fold_in(key, 6)
    for dim, blocks in split:
        heights = jnp.exp(jax.random.uniform(jax.random.fold_in(own, dim), (blocks,), jnp.float32, least / len(split), top_value / len(split)))
        factor_of = factor_of * jnp.repeat(heights, dims[dim] // blocks).reshape([-1 if axis == dim else 1 for axis in range(len(dims))])
    return factor_of


def bell_draw(stream_key, dims, scale, most, split=(), held_as=jnp.bfloat16):
    values = jax.random.normal(stream_key, dims, jnp.float32) * scale
    if len(split) > 0:
        values = steps_of(stream_key, dims, split, -0.22, 0.18) * values
    return jnp.clip(values, min=-most, max=most).astype(held_as)


def setup_inputs(seed: int = 0) -> dict:
    keys = jax.random.split(jax.random.key(seed), 8)
    transition = draw_transition(jax.random.fold_in(keys[7], 71), 0)
    covariance = draw_covariance(jax.random.fold_in(keys[7], 71), 0)
    information = draw_information(jax.random.fold_in(keys[7], 71), 0)
    offset_vec = bell_draw(keys[3], (BLOCKS, N), 1.0, 6.0, ((0, 32), (1, 16)), jnp.float32)
    info_vec = bell_draw(keys[4], (BLOCKS, N), 1.0, 6.0, ((0, 32), (1, 16)), jnp.float32)
    step_counts = plant(jax.random.randint(keys[5], (BLOCKS,), 1, MOST_STEPS + 1), jax.random.fold_in(keys[5], 1), 1, MOST_STEPS).astype(jnp.int32)
    scan_level = jax.random.randint(keys[6], (1,), 0, LEVELS).astype(jnp.int32)
    return {"transition": transition, "covariance": covariance, "information": information, "offset_vec": offset_vec, "info_vec": info_vec, "step_counts": step_counts, "scan_level": scan_level}


def combine_pair(pair_args):
    earlier, later = pair_args
    ptrans, pcovar, poffset, pcount = earlier
    otrans, ocovar, oinform, ooffset, oeta, ocount = later
    identity = jnp.eye(N, dtype=jnp.float32)
    guess_scale = 1.0 / (2.0 + 0.4 * (pcount + ocount).astype(jnp.float32))
    sum_mat = (identity + jnp.dot(pcovar, oinform, preferred_element_type=jnp.float32)).astype(jnp.bfloat16)
    eta_low = oeta.astype(jnp.bfloat16)
    joined = (poffset + jnp.dot(pcovar, eta_low, preferred_element_type=jnp.float32)).astype(jnp.bfloat16)
    iterate = (2.0 * guess_scale * identity - guess_scale * guess_scale * sum_mat.astype(jnp.float32)).astype(jnp.bfloat16)
    for sweep in range(2):
        bracket = (2.0 * identity - jnp.dot(sum_mat, iterate, preferred_element_type=jnp.float32)).astype(jnp.bfloat16)
        iterate = jnp.dot(iterate, bracket, preferred_element_type=jnp.float32).astype(jnp.bfloat16)
    leading = jnp.dot(otrans, iterate, preferred_element_type=jnp.float32).astype(jnp.bfloat16)
    new_trans = jnp.dot(leading, ptrans, preferred_element_type=jnp.float32).astype(jnp.bfloat16)
    right_cov = jnp.dot(leading, pcovar, preferred_element_type=jnp.float32).astype(jnp.bfloat16)
    new_covariance = (jnp.dot(right_cov, otrans.T, preferred_element_type=jnp.float32) + ocovar.astype(jnp.float32)).astype(jnp.bfloat16)
    new_offset = jnp.dot(leading, joined, preferred_element_type=jnp.float32) + ooffset
    return new_trans, new_covariance, new_offset


def reference(transition, covariance, information, offset_vec, info_vec, step_counts, scan_level):
    distance = jnp.left_shift(jnp.int32(1), scan_level[0].astype(jnp.int32))
    positions = jnp.arange(BLOCKS, dtype=jnp.int32)
    earlier = jnp.maximum(positions - distance, 0).astype(jnp.int32)
    has_partner = positions >= distance
    partner = (transition[earlier], covariance[earlier], offset_vec[earlier], step_counts[earlier])
    itself = (transition, covariance, information, offset_vec, info_vec, step_counts)
    new_trans, new_covariance, new_offset = lax.map(combine_pair, (partner, itself))
    new_trans = jnp.where(has_partner[:, None, None], new_trans, transition)
    new_covariance = jnp.where(has_partner[:, None, None], new_covariance, covariance)
    new_offset = jnp.where(has_partner[:, None], new_offset, offset_vec)
    new_counts = jnp.where(has_partner, step_counts[earlier] + step_counts, step_counts)
    return new_trans, new_covariance, new_offset, new_counts
```

```python
import functools
import jax
import jax.numpy as jnp
from jax import lax
from jax.experimental import pallas as pl
from jax.experimental.pallas import tpu as pltpu
from jax.sharding import PartitionSpec as P

F32, BF16 = jnp.float32, jnp.bfloat16
VEC_ROWS = 16
LANES = 128
STRIP = 256


def matmul(a, b):
    return jnp.dot(a, b, preferred_element_type=F32)


def combine_kernel(
    rows, shards,
    scale_ref, trans_ref, covar_ref, gathered,
    trans_out, covar_out, moved_out,
    inform, pcovar, ptrans, otrans, vectors, ratio, panel, joined, sems,
):
    width = trans_ref.shape[1]
    strips = width // STRIP
    wide = vectors.shape[2]
    homes = (inform, pcovar, ptrans, otrans)
    copies = []
    for k, home in enumerate(homes):
        copies.append(pltpu.make_async_copy(gathered.at[:, pl.ds(k * rows, rows), :], home, sems.at[k]))
    copies.append(pltpu.make_async_copy(gathered.at[:, pl.ds(4 * rows, VEC_ROWS), :], vectors, sems.at[4]))
    for k in (0, 1, 4, 2, 3):
        copies[k].start()
    copies[0].wait()
    copies[1].wait()
    scale = scale_ref[0]
    tall = width // 2

    @pl.loop(0, strips)
    def _(s):
        cols = pl.ds(pl.multiple_of(s * STRIP, STRIP), STRIP)
        right = inform[:, :, cols].reshape(width, STRIP)
        for half in range(2):
            left = pcovar[pl.ds(half * shards // 2, shards // 2)].reshape(tall, width)
            unit = (
                lax.broadcasted_iota(jnp.int32, (tall, STRIP), 0) + half * tall
                == lax.broadcasted_iota(jnp.int32, (tall, STRIP), 1) + s * STRIP
            ).astype(F32)
            sum_mat = (unit + matmul(left, right)).astype(BF16).astype(F32)
            ratio[pl.ds(half * tall, tall), cols] = (unit - scale * sum_mat).astype(BF16)

    panel[0] = trans_ref[...]
    for step in range(7):
        now, later = step % 2, (step + 1) % 2
        last = step == 6

        @pl.loop(0, strips)
        def _(s):
            cols = pl.ds(pl.multiple_of(s * STRIP, STRIP), STRIP)
            value = trans_ref[:, cols].astype(F32) + matmul(panel[now], ratio[:, cols])
            if last:
                value = value * scale
            panel[later, :, cols] = value.astype(BF16)

    copies[4].wait()
    eta, offset = [], []
    packed = vectors[...]
    lane = lax.broadcasted_iota(jnp.int32, (rows, wide // (rows // VEC_ROWS)), 1)
    block = wide // (rows // VEC_ROWS)
    for q in range(shards):
        pieces = [packed[q][:, pl_k * block:(pl_k + 1) * block] for pl_k in range(rows // VEC_ROWS)]
        whole = jnp.concatenate(pieces, axis=0)
        offset.append(
            jnp.sum(jnp.where((lane >= 1) & (lane <= 3), whole.astype(F32), 0.0), axis=1, keepdims=True)
        )
        joined[pl.ds(q * rows, rows), :] = jnp.where(lane == 0, whole.astype(F32), 0.0).astype(BF16)
    eta = joined[...]
    for half in range(2):
        left = pcovar[pl.ds(half * shards // 2, shards // 2)].reshape(tall, width)
        moved = matmul(left, eta)
        base = jnp.concatenate(offset[half * shards // 2:(half + 1) * shards // 2], axis=0)
        lane_t = lax.broadcasted_iota(jnp.int32, (tall, block), 1)
        joined[pl.ds(half * tall, tall), :] = jnp.where(lane_t == 0, moved + base, 0.0).astype(BF16)
    moved_out[...] = matmul(panel[1], joined[...])

    copies[2].wait()

    @pl.loop(0, strips)
    def _(s):
        cols = pl.ds(pl.multiple_of(s * STRIP, STRIP), STRIP)
        right = pcovar[:, :, cols].reshape(width, STRIP)
        panel[0, :, cols] = matmul(panel[1], right).astype(BF16)
        trans_out[:, cols] = matmul(panel[1], ptrans[:, :, cols].reshape(width, STRIP)).astype(BF16)

    copies[3].wait()
    moved = lax.dot_general(
        panel[0], otrans[...].reshape(width, width), (((1,), (1,)), ((), ())), preferred_element_type=F32
    )
    covar_out[...] = (moved + covar_ref[...].astype(F32)).astype(BF16)


def combine(scale, trans, covar, gathered):
    rows, width = trans.shape
    shards = gathered.shape[0]
    block = width // (rows // VEC_ROWS)
    vmem = pl.BlockSpec(memory_space=pltpu.VMEM)
    mat = pltpu.VMEM((shards, rows, width), BF16)
    return pl.pallas_call(
        functools.partial(combine_kernel, rows, shards),
        out_shape=(
            jax.ShapeDtypeStruct((rows, width), BF16),
            jax.ShapeDtypeStruct((rows, width), BF16),
            jax.ShapeDtypeStruct((rows, block), F32),
        ),
        in_specs=[pl.BlockSpec(memory_space=pltpu.SMEM), vmem, vmem, pl.BlockSpec(memory_space=pl.ANY)],
        out_specs=(vmem, vmem, vmem),
        scratch_shapes=[
            mat, mat, mat, mat,
            pltpu.VMEM((shards, VEC_ROWS, width), BF16),
            pltpu.VMEM((width, width), BF16),
            pltpu.VMEM((2, rows, width), BF16),
            pltpu.VMEM((width, block), BF16),
            pltpu.SemaphoreType.DMA((5,)),
        ],
        compiler_params=pltpu.CompilerParams(vmem_limit_bytes=48 * 2**20),
        name="combine",
    )(scale, trans, covar, gathered)


def spread_vectors(columns, rows, width):
    parts = rows // VEC_ROWS
    block = width // parts
    stacked = jnp.stack(columns, axis=1)
    whole = jnp.pad(stacked, ((0, 0), (0, block - stacked.shape[1])))
    return whole.reshape(parts, VEC_ROWS, block).transpose(1, 0, 2).reshape(VEC_ROWS, width)


def thirds(vector):
    high = vector.astype(BF16)
    rest = vector - high.astype(F32)
    middle = rest.astype(BF16)
    low = (rest - middle.astype(F32)).astype(BF16)
    return high, middle, low


def from_behind(block, axis, distance):
    devices = range(lax.axis_size(axis))
    route = [(i - distance, i) for i in devices if i - distance in devices]
    return lax.ppermute(block, axis, route)


def local(transition, covariance, information, offset_vec, info_vec, step_counts, scan_level):
    rows, width = transition.shape[1:]
    trans, covar, inform = transition[0], covariance[0], information[0]
    offset = offset_vec[0]
    count = step_counts.astype(F32)
    nothing = jnp.zeros((rows,), BF16)
    high, middle, low = thirds(offset)
    counts = jnp.broadcast_to(count.astype(BF16), (rows,))
    sent_vectors = spread_vectors([nothing, high, middle, low, counts], rows, width)
    own_vectors = spread_vectors([info_vec[0].astype(BF16)], rows, width)
    sent = jnp.concatenate([covar, trans, sent_vectors], axis=0)
    levels = lax.axis_size("tm").bit_length() - 1
    branches = [functools.partial(from_behind, axis="tm", distance=2**k) for k in range(levels)]
    got = lax.switch(scan_level[0], branches, sent)
    part_count = got[2 * rows, 4:5].astype(F32)
    scale = 1.0 / (2.0 + 0.4 * (part_count + count))
    packed = jnp.concatenate(
        [inform, got[: 2 * rows], trans, got[2 * rows :] + own_vectors], axis=0
    )
    gathered = lax.all_gather(packed, "state", axis=0, tiled=False)
    new_trans, new_covariance, moved = combine(scale, trans, covar, gathered)
    new_offset = moved[:, 0] + offset
    distance = jnp.left_shift(jnp.int32(1), scan_level[0])
    has_partner = lax.axis_index("tm") >= distance
    new_trans = jnp.where(has_partner, new_trans, trans)
    new_covariance = jnp.where(has_partner, new_covariance, covar)
    new_offset = jnp.where(has_partner, new_offset, offset)
    new_counts = jnp.where(has_partner, part_count + count, count).astype(jnp.int32)
    return (new_trans[None], new_covariance[None], new_offset[None], new_counts)


def solution(mesh):
    in_specs = (
        P("tm", "state", None),
        P("tm", "state", None),
        P("tm", "state", None),
        P("tm", "state"),
        P("tm", "state"),
        P("tm"),
        P(),
    )
    out_specs = (P("tm", "state", None), P("tm", "state", None), P("tm", "state"), P("tm"))
    return jax.shard_map(local, mesh=mesh, in_specs=in_specs, out_specs=out_specs, check_vma=False)
```

```python
import jax
import jax.numpy as jnp
from jax import lax
from jax.experimental import pallas as pl
from jax.experimental.pallas import tpu as pltpu
from jax.sharding import PartitionSpec as P

F32, BF16, F16 = jnp.float32, jnp.bfloat16, jnp.float16
NOTE_ROWS = 16
STRIP = 256
BASE = 2.0**12
STEP = 2.0**16
STEPS = 7
ETA, ETA_GRADE, INFORM_GRADE, OWN_TRANS_GRADE = 0, 1, 2, 3
OFFSET, OFFSET_GRADE, COVAR_GRADE, TRANS_GRADE, COUNT = 4, 7, 8, 9, 10

VMEM = pl.BlockSpec(memory_space=pltpu.VMEM)
SMEM = pl.BlockSpec(memory_space=pltpu.SMEM)
ANY = pl.BlockSpec(memory_space=pl.ANY)


def matmul(a, b):
    return jnp.dot(a, b, preferred_element_type=F32)


def times_transpose(a, b):
    return lax.dot_general(a, b, (((1,), (1,)), ((), ())), preferred_element_type=F32)


def graded(value):
    peak = jnp.max(jnp.max(jnp.abs(value), axis=1, keepdims=True), axis=0, keepdims=True)
    factor, grade = jnp.full((1, 1), BASE, F32), jnp.zeros((1, 1), F32)
    for k in range(1, STEPS + 1):
        small = peak < STEP**-k
        factor = jnp.where(small, factor * STEP, factor)
        grade = jnp.where(small, grade + 1.0, grade)
    return factor, grade


def inverse(grade):
    factor = jnp.full(grade.shape, 1.0 / BASE, F32)
    for k in range(1, STEPS + 1):
        factor = jnp.where(grade >= k, factor * (1.0 / STEP), factor)
    return factor


def pack_kernel(trans_ref, covar_ref, inform_ref, offset_ref, eta_ref, count_ref, sent_ref, own_ref):
    rows, width = trans_ref.shape

    def put(target, first, value_ref):
        value = value_ref[...].astype(F32)
        factor, grade = graded(value)
        target[first : first + rows, :] = (value * factor).astype(BF16)
        return jnp.broadcast_to(grade, (1, rows))

    covar_grade = put(sent_ref, 0, covar_ref)
    trans_grade = put(sent_ref, rows, trans_ref)
    inform_grade = put(own_ref, 0, inform_ref)
    own_ref[rows : 2 * rows, :] = sent_ref[rows : 2 * rows, :]
    eta = eta_ref[...].astype(BF16).astype(F32)
    eta_factor, eta_grade = graded(eta)
    offset = offset_ref[...]
    offset_factor, offset_grade = graded(offset)
    offset = offset * offset_factor
    parts = []
    for _ in range(3):
        part = offset.astype(BF16).astype(F32)
        parts.append(part)
        offset = offset - part
    one = jnp.ones((1, rows), F32)
    own_notes = [eta * eta_factor, one * eta_grade, inform_grade, trans_grade]
    count = one * count_ref[0].astype(F32)
    sent_notes = parts + [one * offset_grade, covar_grade, trans_grade, count]

    def notes(first, given):
        index = lax.broadcasted_iota(jnp.int32, (NOTE_ROWS, rows), 0)
        total = jnp.zeros((NOTE_ROWS, rows), F32)
        for k, row in enumerate(given):
            total = jnp.where(index == first + k, row, total)
        return total.astype(BF16)

    for target, first, given in ((own_ref, ETA, own_notes), (sent_ref, OFFSET, sent_notes)):
        target[2 * rows :, :] = jnp.zeros((NOTE_ROWS, width), BF16)
        target[2 * rows :, :rows] = notes(first, given)


def pack(trans, covar, inform, offset, eta, count):
    rows, width = trans.shape
    packed = jax.ShapeDtypeStruct((2 * rows + NOTE_ROWS, width), BF16)
    return pl.pallas_call(
        pack_kernel,
        out_shape=(packed, packed),
        in_specs=[VMEM] * 5 + [SMEM],
        out_specs=(VMEM, VMEM),
        name="pack",
    )(trans, covar, inform, offset, eta, count)


def combine_kernel(
    count_ref, trans_ref, covar_ref, offset_ref, notes_ref, inform_hbm, pcovar_hbm, ptrans_hbm, otrans_hbm,
    trans_out, covar_out, offset_out, count_out,
    inform, pcovar, ptrans, otrans, scaled, inner, lead, panel, sems,
):
    rows, width = trans_ref.shape
    strips = width // STRIP
    tall = width // 2
    pairs = ((inform_hbm, inform), (pcovar_hbm, pcovar), (ptrans_hbm, ptrans), (otrans_hbm, otrans))
    copies = [pltpu.make_async_copy(src, dst, sems.at[k]) for k, (src, dst) in enumerate(pairs)]
    for k in (1, 0, 2, 3):
        copies[k].start()

    def note(row):
        return notes_ref[row : row + 1, :]

    count = count_ref[0].astype(F32)
    part_count = note(COUNT)
    has_partner = jnp.max(part_count) > 0.0
    count_out[0] = (jnp.max(part_count) + count).astype(jnp.int32)
    scale = 1.0 / (2.0 + 0.4 * (part_count + count))
    covar_unit = inverse(note(COVAR_GRADE))
    inform_unit = inverse(note(INFORM_GRADE))

    copies[1].wait()
    for part in range(4):
        some = pl.ds(part * (width // 4), width // 4)
        scaled[some, :] = (pcovar[some, :].astype(F32) * inform_unit).astype(BF16)
    copies[0].wait()

    @pl.loop(0, strips)
    def _(s):
        cols = pl.ds(pl.multiple_of(s * STRIP, STRIP), STRIP)
        for half in range(2):
            part = pl.ds(half * tall, tall)
            inner[part, cols] = matmul(scaled[part, :], inform[:, cols]).astype(BF16)

    lead[0] = trans_ref[...].astype(F32)

    @pl.loop(0, 7)
    def _(step):
        now = lax.rem(step, 2)
        panel[0] = (lead[now] * covar_unit).astype(BF16)
        for s in range(strips):
            cols = slice(s * STRIP, (s + 1) * STRIP)
            moved = matmul(panel[0], inner[:, cols])
            rest = lead[now, :, cols]
            value = trans_ref[:, cols].astype(F32) + rest - scale[:, cols] * (rest + moved)
            lead[1 - now, :, cols] = value

    leading = (lead[1] * scale).astype(BF16)
    plain = leading.astype(F32)
    panel[0] = (plain * covar_unit).astype(BF16)
    panel[1] = (plain * inverse(note(TRANS_GRADE))).astype(BF16)
    for s in range(strips):
        cols = slice(s * STRIP, (s + 1) * STRIP)
        panel[2, :, cols] = matmul(panel[0], pcovar[:, cols]).astype(BF16)
    copies[2].wait()
    for s in range(strips):
        cols = slice(s * STRIP, (s + 1) * STRIP)
        moved = matmul(panel[1], ptrans[:, cols]).astype(BF16)
        trans_out[:, cols] = jnp.where(has_partner, moved, trans_ref[:, cols])

    offset_unit = inverse(note(OFFSET_GRADE))
    eta = notes_ref[ETA : ETA + 1, :] * inverse(note(ETA_GRADE))
    row = lax.broadcasted_iota(jnp.int32, (NOTE_ROWS, 1), 0)
    parts = jnp.where((row >= OFFSET) & (row < OFFSET + 3), notes_ref[...] * offset_unit, 0.0)
    etas = jnp.where(row == ETA, jnp.broadcast_to(eta, parts.shape), 0.0)
    moved = times_transpose(parts.astype(BF16), leading) + times_transpose(etas.astype(BF16), panel[2])
    moved = jnp.sum(moved, axis=0, keepdims=True)
    offset_out[...] = jnp.where(has_partner, moved + offset_ref[...], offset_ref[...])

    copies[3].wait()
    own_trans_unit = inverse(note(OWN_TRANS_GRADE))
    for s in range(strips):
        cols = slice(s * STRIP, (s + 1) * STRIP)
        moved = times_transpose(panel[2], otrans[cols, :]) * own_trans_unit[:, cols]
        own = covar_ref[:, cols]
        covar_out[:, cols] = jnp.where(has_partner, (moved + own.astype(F32)).astype(BF16), own)


def combine(count, trans, covar, offset, notes, matrices):
    rows, width = trans.shape
    mat = pltpu.VMEM((width, width), BF16)
    panel = jax.ShapeDtypeStruct((rows, width), BF16)
    return pl.pallas_call(
        combine_kernel,
        out_shape=(
            panel,
            panel,
            jax.ShapeDtypeStruct(offset.shape, F32),
            jax.ShapeDtypeStruct((1,), jnp.int32),
        ),
        in_specs=[SMEM] + [VMEM] * 4 + [ANY] * 4,
        out_specs=(VMEM, VMEM, VMEM, SMEM),
        scratch_shapes=[
            mat, mat, mat, mat, mat, mat,
            pltpu.VMEM((2, rows, width), F32),
            pltpu.VMEM((3, rows, width), BF16),
            pltpu.SemaphoreType.DMA((4,)),
        ],
        compiler_params=pltpu.CompilerParams(vmem_limit_bytes=48 * 2**20),
        name="combine",
    )(count, trans, covar, offset, notes, *matrices)


def fetch_at(distance):

    def fetch(operand):
        sent, own = operand
        devices = range(lax.axis_size("tm"))
        route = [(i - distance, i) for i in devices if i - distance in devices]
        got = lax.ppermute(sent, "tm", route)
        return got, lax.all_gather(own, "state")

    return fetch


def local(transition, covariance, information, offset_vec, info_vec, step_counts, scan_level):
    rows, width = transition.shape[1:]
    trans, covar = transition[0], covariance[0]
    sent, own = pack(trans, covar, information[0], offset_vec, info_vec, step_counts)
    levels = lax.axis_size("tm").bit_length() - 1
    branches = [fetch_at(2**k) for k in range(levels)]
    got, mine = lax.switch(scan_level[0], branches, (sent.astype(F16), own.astype(F16)))
    theirs = lax.all_gather(got, "state")

    def matrix(gathered, place):
        return gathered[:, place * rows : (place + 1) * rows].astype(BF16).reshape(width, width)

    def notes(gathered):
        return gathered[:, 2 * rows :, :rows].astype(F32).transpose(1, 0, 2).reshape(NOTE_ROWS, width)

    matrices = (matrix(mine, 0), matrix(theirs, 0), matrix(theirs, 1), matrix(mine, 1))
    new_trans, new_covariance, new_offset, new_counts = combine(
        step_counts, trans, covar, offset_vec, notes(mine) + notes(theirs), matrices
    )
    return (new_trans[None], new_covariance[None], new_offset, new_counts)


def solution(mesh):
    in_specs = (
        P("tm", "state", None),
        P("tm", "state", None),
        P("tm", "state", None),
        P("tm", "state"),
        P("tm", "state"),
        P("tm"),
        P(),
    )
    out_specs = (P("tm", "state", None), P("tm", "state", None), P("tm", "state"), P("tm"))
    return jax.shard_map(local, mesh=mesh, in_specs=in_specs, out_specs=out_specs, check_vma=False)
```

```python
import jax
import jax.numpy as jnp
from jax import lax
from jax.experimental import pallas as pl
from jax.experimental.pallas import tpu as pltpu
from jax.sharding import PartitionSpec as P

F32, BF16, F16 = jnp.float32, jnp.bfloat16, jnp.float16
NOTE_ROWS = 8
ALL_NOTES = 2 * NOTE_ROWS
STRIP = 256
BASE = 2.0**12
STEP = 2.0**16
STEPS = 7
ETA, ETA_GRADE, INFORM_GRADE, OWN_TRANS_GRADE = 0, 1, 2, 3
OFFSET, OFFSET_GRADE, COVAR_GRADE, TRANS_GRADE, COUNT = 8, 11, 12, 13, 14

VMEM = pl.BlockSpec(memory_space=pltpu.VMEM)
SMEM = pl.BlockSpec(memory_space=pltpu.SMEM)
ANY = pl.BlockSpec(memory_space=pl.ANY)


def matmul(a, b):
    return jnp.dot(a, b, preferred_element_type=F32)


def times_transpose(a, b):
    return lax.dot_general(a, b, (((1,), (1,)), ((), ())), preferred_element_type=F32)


def graded(value):
    peak = jnp.max(jnp.max(jnp.abs(value), axis=1, keepdims=True), axis=0, keepdims=True)
    factor, grade = jnp.full((1, 1), BASE, F32), jnp.zeros((1, 1), F32)
    for k in range(1, STEPS + 1):
        small = peak < STEP**-k
        factor = jnp.where(small, factor * STEP, factor)
        grade = jnp.where(small, grade + 1.0, grade)
    return factor, grade


def inverse(grade):
    factor = jnp.full(grade.shape, 1.0 / BASE, F32)
    for k in range(1, STEPS + 1):
        factor = jnp.where(grade >= k, factor * (1.0 / STEP), factor)
    return factor


def pack_kernel(trans_ref, covar_ref, inform_ref, offset_ref, eta_ref, count_ref, sent_ref, own_ref, notes_ref):
    rows, width = trans_ref.shape

    def put(target, first, value_ref):
        value = value_ref[...].astype(F32)
        factor, grade = graded(value)
        target[first : first + rows, :] = (value * factor).astype(BF16)
        return jnp.broadcast_to(grade, (1, rows))

    covar_grade = put(sent_ref, 0, covar_ref)
    trans_grade = put(sent_ref, rows, trans_ref)
    inform_grade = put(own_ref, 0, inform_ref)
    own_ref[rows : 2 * rows, :] = sent_ref[rows : 2 * rows, :]
    eta = eta_ref[...].astype(BF16).astype(F32)
    eta_factor, eta_grade = graded(eta)
    offset = offset_ref[...]
    offset_factor, offset_grade = graded(offset)
    offset = offset * offset_factor
    parts = []
    for _ in range(3):
        part = offset.astype(BF16).astype(F32)
        parts.append(part)
        offset = offset - part
    one = jnp.ones((1, rows), F32)
    own_notes = [eta * eta_factor, one * eta_grade, inform_grade, trans_grade]
    count = one * count_ref[0].astype(F32)
    sent_notes = parts + [one * offset_grade, covar_grade, trans_grade, count]

    index = lax.broadcasted_iota(jnp.int32, (ALL_NOTES, rows), 0)
    total = jnp.zeros((ALL_NOTES, rows), F32)
    for first, given in ((ETA, own_notes), (OFFSET, sent_notes)):
        for k, row in enumerate(given):
            total = jnp.where(index == first + k, row, total)
    notes_ref[...] = jnp.zeros((ALL_NOTES, width), BF16)
    notes_ref[:, :rows] = total.astype(BF16)


def pack(trans, covar, inform, offset, eta, count):
    rows, width = trans.shape
    packed = jax.ShapeDtypeStruct((2 * rows, width), BF16)
    return pl.pallas_call(
        pack_kernel,
        out_shape=(packed, packed, jax.ShapeDtypeStruct((ALL_NOTES, width), BF16)),
        in_specs=[VMEM] * 5 + [SMEM],
        out_specs=(VMEM, VMEM, VMEM),
        name="pack",
    )(trans, covar, inform, offset, eta, count)


def combine_kernel(
    count_ref, trans_ref, covar_ref, offset_ref, notes_ref, inform, pcovar, ptrans_hbm, otrans_hbm,
    trans_out, covar_out, offset_out, count_out,
    ptrans, otrans, scaled, inner, lead, panel, sems,
):
    rows, width = trans_ref.shape
    strips = width // STRIP
    tall = width // 2
    copies = [
        pltpu.make_async_copy(ptrans_hbm, ptrans, sems.at[0]),
        pltpu.make_async_copy(otrans_hbm, otrans, sems.at[1]),
    ]
    for copy in copies:
        copy.start()

    def note(row):
        return notes_ref[row : row + 1, :]

    count = count_ref[0].astype(F32)
    part_count = note(COUNT)
    has_partner = jnp.max(part_count) > 0.0
    count_out[0] = (jnp.max(part_count) + count).astype(jnp.int32)
    scale = 1.0 / (2.0 + 0.4 * (part_count + count))
    covar_unit = inverse(note(COVAR_GRADE))
    inform_unit = inverse(note(INFORM_GRADE))

    for part in range(4):
        some = pl.ds(part * (width // 4), width // 4)
        scaled[some, :] = (pcovar[some, :].astype(F32) * inform_unit).astype(BF16)

    @pl.loop(0, strips)
    def _(s):
        cols = pl.ds(pl.multiple_of(s * STRIP, STRIP), STRIP)
        for half in range(2):
            part = pl.ds(half * tall, tall)
            inner[part, cols] = matmul(scaled[part, :], inform[:, cols]).astype(BF16)

    lead[0] = trans_ref[...].astype(F32)

    @pl.loop(0, 7)
    def _(step):
        now = lax.rem(step, 2)
        panel[0] = (lead[now] * covar_unit).astype(BF16)
        for s in range(strips):
            cols = slice(s * STRIP, (s + 1) * STRIP)
            moved = matmul(panel[0], inner[:, cols])
            rest = lead[now, :, cols]
            value = trans_ref[:, cols].astype(F32) + rest - scale[:, cols] * (rest + moved)
            lead[1 - now, :, cols] = value

    leading = (lead[1] * scale).astype(BF16)
    plain = leading.astype(F32)
    panel[0] = (plain * covar_unit).astype(BF16)
    panel[1] = (plain * inverse(note(TRANS_GRADE))).astype(BF16)
    for s in range(strips):
        cols = slice(s * STRIP, (s + 1) * STRIP)
        panel[2, :, cols] = matmul(panel[0], pcovar[:, cols]).astype(BF16)
    copies[0].wait()
    for s in range(strips):
        cols = slice(s * STRIP, (s + 1) * STRIP)
        moved = matmul(panel[1], ptrans[:, cols]).astype(BF16)
        trans_out[:, cols] = jnp.where(has_partner, moved, trans_ref[:, cols])

    offset_unit = inverse(note(OFFSET_GRADE))
    eta = notes_ref[ETA : ETA + 1, :] * inverse(note(ETA_GRADE))
    row = lax.broadcasted_iota(jnp.int32, (ALL_NOTES, 1), 0)
    parts = jnp.where((row >= OFFSET) & (row < OFFSET + 3), notes_ref[...] * offset_unit, 0.0)
    etas = jnp.where(row == ETA, jnp.broadcast_to(eta, parts.shape), 0.0)
    moved = times_transpose(parts.astype(BF16), leading) + times_transpose(etas.astype(BF16), panel[2])
    moved = jnp.sum(moved, axis=0, keepdims=True)
    offset_out[...] = jnp.where(has_partner, moved + offset_ref[...], offset_ref[...])

    copies[1].wait()
    own_trans_unit = inverse(note(OWN_TRANS_GRADE))
    for s in range(strips):
        cols = slice(s * STRIP, (s + 1) * STRIP)
        moved = times_transpose(panel[2], otrans[cols, :]) * own_trans_unit[:, cols]
        own = covar_ref[:, cols]
        covar_out[:, cols] = jnp.where(has_partner, (moved + own.astype(F32)).astype(BF16), own)


def combine(count, trans, covar, offset, notes, matrices):
    rows, width = trans.shape
    mat = pltpu.VMEM((width, width), BF16)
    panel = jax.ShapeDtypeStruct((rows, width), BF16)
    return pl.pallas_call(
        combine_kernel,
        out_shape=(
            panel,
            panel,
            jax.ShapeDtypeStruct(offset.shape, F32),
            jax.ShapeDtypeStruct((1,), jnp.int32),
        ),
        in_specs=[SMEM] + [VMEM] * 6 + [ANY] * 2,
        out_specs=(VMEM, VMEM, VMEM, SMEM),
        scratch_shapes=[
            mat, mat, mat, mat,
            pltpu.VMEM((2, rows, width), F32),
            pltpu.VMEM((3, rows, width), BF16),
            pltpu.SemaphoreType.DMA((2,)),
        ],
        compiler_params=pltpu.CompilerParams(vmem_limit_bytes=48 * 2**20),
        name="combine",
    )(count, trans, covar, offset, notes, *matrices)


def fetch_at(distance):

    def fetch(operand):
        sent, own = operand
        devices = range(lax.axis_size("tm"))
        route = [(i - distance, i) for i in devices if i - distance in devices]
        got = lax.ppermute(sent, "tm", route)
        return got, lax.all_gather(own, "state")

    return fetch


def local(transition, covariance, information, offset_vec, info_vec, step_counts, scan_level):
    rows, width = transition.shape[1:]
    trans, covar = transition[0], covariance[0]
    sent, own, own_notes = pack(trans, covar, information[0], offset_vec, info_vec, step_counts)
    sent = jnp.concatenate([sent, own_notes[NOTE_ROWS:]]).astype(F16)
    own = jnp.concatenate([own, own_notes[:NOTE_ROWS]]).astype(F16)
    levels = lax.axis_size("tm").bit_length() - 1
    branches = [fetch_at(2**k) for k in range(levels)]
    got, mine = lax.switch(scan_level[0], branches, (sent, own))
    theirs = lax.all_gather(got, "state")

    def matrix(gathered, place):
        return gathered[:, place * rows : (place + 1) * rows].astype(BF16).reshape(width, width)

    def notes(gathered):
        return gathered[:, 2 * rows :, :rows].astype(F32).transpose(1, 0, 2).reshape(NOTE_ROWS, width)

    matrices = (matrix(mine, 0), matrix(theirs, 0), matrix(theirs, 1), matrix(mine, 1))
    new_trans, new_covariance, new_offset, new_counts = combine(
        step_counts, trans, covar, offset_vec, jnp.concatenate([notes(mine), notes(theirs)]), matrices
    )
    return (new_trans[None], new_covariance[None], new_offset, new_counts)


def solution(mesh):
    in_specs = (
        P("tm", "state", None),
        P("tm", "state", None),
        P("tm", "state", None),
        P("tm", "state"),
        P("tm", "state"),
        P("tm"),
        P(),
    )
    out_specs = (P("tm", "state", None), P("tm", "state", None), P("tm", "state"), P("tm"))
    return jax.shard_map(local, mesh=mesh, in_specs=in_specs, out_specs=out_specs, check_vma=False)
```

```python
import jax
import jax.numpy as jnp
from jax import lax
from jax.experimental import pallas as pl
from jax.experimental.pallas import tpu as pltpu
from jax.sharding import PartitionSpec as P

F32, BF16, F16 = jnp.float32, jnp.bfloat16, jnp.float16
NOTE_ROWS = 8
PACKED_ROWS = 16
STRIP = 256
BASE = 2.0**12
STEP = 2.0**16
STEPS = 7
ETA, ETA_GRADE, INFORM_GRADE, OWN_TRANS_GRADE = 0, 1, 2, 3
OFFSET_GRADE, COVAR_GRADE, TRANS_GRADE, COUNT = 3, 4, 5, 6

VMEM = pl.BlockSpec(memory_space=pltpu.VMEM)
SMEM = pl.BlockSpec(memory_space=pltpu.SMEM)
ANY = pl.BlockSpec(memory_space=pl.ANY)


def matmul(a, b):
    return jnp.dot(a, b, preferred_element_type=F32)


def times_transpose(a, b):
    return lax.dot_general(a, b, (((1,), (1,)), ((), ())), preferred_element_type=F32)


def graded(value):
    peak = jnp.max(jnp.max(jnp.abs(value), axis=1, keepdims=True), axis=0, keepdims=True)
    factor, grade = jnp.full((1, 1), BASE, F32), jnp.zeros((1, 1), F32)
    for k in range(1, STEPS + 1):
        small = peak < STEP**-k
        factor = jnp.where(small, factor * STEP, factor)
        grade = jnp.where(small, grade + 1.0, grade)
    return factor, grade


def inverse(grade):
    factor = jnp.full(grade.shape, 1.0 / BASE, F32)
    for k in range(1, STEPS + 1):
        factor = jnp.where(grade >= k, factor * (1.0 / STEP), factor)
    return factor


def pack_kernel(trans_ref, covar_ref, inform_ref, offset_ref, eta_ref, count_ref, sent_ref, own_ref):
    rows, width = trans_ref.shape

    def put(target, first, value_ref):
        value = value_ref[...].astype(F32)
        factor, grade = graded(value)
        target[first : first + rows, :] = (value * factor).astype(BF16)
        return jnp.broadcast_to(grade, (1, rows))

    covar_grade = put(sent_ref, 0, covar_ref)
    trans_grade = put(sent_ref, rows, trans_ref)
    inform_grade = put(own_ref, 0, inform_ref)
    own_ref[rows : 2 * rows, :] = sent_ref[rows : 2 * rows, :]
    eta = eta_ref[...].astype(BF16).astype(F32)
    eta_factor, eta_grade = graded(eta)
    offset = offset_ref[...]
    offset_factor, offset_grade = graded(offset)
    offset = offset * offset_factor
    parts = []
    for _ in range(3):
        part = offset.astype(BF16).astype(F32)
        parts.append(part)
        offset = offset - part
    one = jnp.ones((1, rows), F32)
    own_notes = [eta * eta_factor, one * eta_grade, inform_grade, trans_grade]
    count = one * count_ref[0].astype(F32)
    sent_notes = parts + [one * offset_grade, covar_grade, trans_grade, count]

    index = lax.broadcasted_iota(jnp.int32, (PACKED_ROWS, rows), 0)
    for target, given in ((own_ref, own_notes), (sent_ref, sent_notes)):
        total = jnp.zeros((PACKED_ROWS, rows), F32)
        for k, row in enumerate(given):
            total = jnp.where(index == k, row, total)
        target[2 * rows :, :] = jnp.zeros((PACKED_ROWS, width), BF16)
        target[2 * rows :, :rows] = total.astype(BF16)


def pack(trans, covar, inform, offset, eta, count):
    rows, width = trans.shape
    packed = jax.ShapeDtypeStruct((2 * rows + PACKED_ROWS, width), BF16)
    return pl.pallas_call(
        pack_kernel,
        out_shape=(packed, packed),
        in_specs=[VMEM] * 5 + [SMEM],
        out_specs=(VMEM, VMEM),
        name="pack",
    )(trans, covar, inform, offset, eta, count)


def combine_kernel(
    count_ref, trans_ref, covar_ref, offset_ref, both_ref,
    inform_hbm, pcovar_hbm, ptrans_hbm, otrans_hbm,
    trans_out, covar_out, offset_out, count_out,
    inform, pcovar, ptrans, otrans, scaled, inner, lead, panel, sems,
):
    rows, width = trans_ref.shape
    strips = width // STRIP
    tall = width // 2
    pairs = ((pcovar_hbm, pcovar), (inform_hbm, inform), (ptrans_hbm, ptrans), (otrans_hbm, otrans))
    copies = [pltpu.make_async_copy(src, dst, sems.at[k]) for k, (src, dst) in enumerate(pairs)]
    for copy in copies:
        copy.start()

    def own_note(row):
        return both_ref[row : row + 1, :]

    def note(row):
        return both_ref[NOTE_ROWS + row : NOTE_ROWS + row + 1, :]

    count = count_ref[0].astype(F32)
    part_count = note(COUNT)
    has_partner = jnp.max(part_count) > 0.0
    count_out[0] = (jnp.max(part_count) + count).astype(jnp.int32)
    scale = 1.0 / (2.0 + 0.4 * (part_count + count))
    covar_unit = inverse(note(COVAR_GRADE))
    inform_unit = inverse(own_note(INFORM_GRADE))

    copies[0].wait()
    for part in range(4):
        some = pl.ds(part * (width // 4), width // 4)
        scaled[some, :] = (pcovar[some, :].astype(F32) * inform_unit).astype(BF16)

    copies[1].wait()

    @pl.loop(0, strips)
    def _(s):
        cols = pl.ds(pl.multiple_of(s * STRIP, STRIP), STRIP)
        for half in range(2):
            part = pl.ds(half * tall, tall)
            inner[part, cols] = matmul(scaled[part, :], inform[:, cols]).astype(BF16)

    lead[0] = trans_ref[...].astype(F32)

    @pl.loop(0, 7)
    def _(step):
        now = lax.rem(step, 2)
        panel[0] = (lead[now] * covar_unit).astype(BF16)
        for s in range(strips):
            cols = slice(s * STRIP, (s + 1) * STRIP)
            moved = matmul(panel[0], inner[:, cols])
            rest = lead[now, :, cols]
            value = trans_ref[:, cols].astype(F32) + rest - scale[:, cols] * (rest + moved)
            lead[1 - now, :, cols] = value

    leading = (lead[1] * scale).astype(BF16)
    plain = leading.astype(F32)
    panel[0] = (plain * covar_unit).astype(BF16)
    panel[1] = (plain * inverse(note(TRANS_GRADE))).astype(BF16)
    for s in range(strips):
        cols = slice(s * STRIP, (s + 1) * STRIP)
        panel[2, :, cols] = matmul(panel[0], pcovar[:, cols]).astype(BF16)
    copies[2].wait()
    for s in range(strips):
        cols = slice(s * STRIP, (s + 1) * STRIP)
        moved = matmul(panel[1], ptrans[:, cols]).astype(BF16)
        trans_out[:, cols] = jnp.where(has_partner, moved, trans_ref[:, cols])

    offset_unit = inverse(note(OFFSET_GRADE))
    eta = own_note(ETA) * inverse(own_note(ETA_GRADE))
    row = lax.broadcasted_iota(jnp.int32, (NOTE_ROWS, 1), 0)
    parts = jnp.where(row < OFFSET_GRADE, both_ref[NOTE_ROWS:, :] * offset_unit, 0.0)
    etas = jnp.where(row == 0, jnp.broadcast_to(eta, parts.shape), 0.0)
    nothing = jnp.zeros(parts.shape, F32)
    moved = times_transpose(jnp.concatenate([parts, nothing]).astype(BF16), leading)
    moved += times_transpose(jnp.concatenate([etas, nothing]).astype(BF16), panel[2])
    moved = jnp.sum(moved, axis=0, keepdims=True)
    offset_out[...] = jnp.where(has_partner, moved + offset_ref[...], offset_ref[...])

    copies[3].wait()
    own_trans_unit = inverse(own_note(OWN_TRANS_GRADE))
    for s in range(strips):
        cols = slice(s * STRIP, (s + 1) * STRIP)
        moved = times_transpose(panel[2], otrans[cols, :]) * own_trans_unit[:, cols]
        own = covar_ref[:, cols]
        covar_out[:, cols] = jnp.where(has_partner, (moved + own.astype(F32)).astype(BF16), own)


def combine(count, trans, covar, offset, both, matrices):
    rows, width = trans.shape
    mat = pltpu.VMEM((width, width), BF16)
    panel = jax.ShapeDtypeStruct((rows, width), BF16)
    return pl.pallas_call(
        combine_kernel,
        out_shape=(
            panel,
            panel,
            jax.ShapeDtypeStruct(offset.shape, F32),
            jax.ShapeDtypeStruct((1,), jnp.int32),
        ),
        in_specs=[SMEM] + [VMEM] * 4 + [ANY] * 4,
        out_specs=(VMEM, VMEM, VMEM, SMEM),
        scratch_shapes=[
            mat, mat, mat, mat, mat, mat,
            pltpu.VMEM((2, rows, width), F32),
            pltpu.VMEM((3, rows, width), BF16),
            pltpu.SemaphoreType.DMA((4,)),
        ],
        compiler_params=pltpu.CompilerParams(vmem_limit_bytes=48 * 2**20),
        name="combine",
    )(count, trans, covar, offset, both, *matrices)


def fetch_at(distance):

    def fetch(operand):
        sent, own = operand
        devices = range(lax.axis_size("tm"))
        route = [(i - distance, i) for i in devices if i - distance in devices]
        got = lax.ppermute(sent, "tm", route)
        return got, lax.all_gather(own, "state")

    return fetch


def local(transition, covariance, information, offset_vec, info_vec, step_counts, scan_level):
    rows, width = transition.shape[1:]
    trans, covar = transition[0], covariance[0]
    sent, own = pack(trans, covar, information[0], offset_vec, info_vec, step_counts)
    kept = 2 * rows + NOTE_ROWS
    sent, own = sent[:kept].astype(F16), own[:kept].astype(F16)
    levels = lax.axis_size("tm").bit_length() - 1
    branches = [fetch_at(2**k) for k in range(levels)]
    got, mine = lax.switch(scan_level[0], branches, (sent, own))
    theirs = lax.all_gather(got, "state")

    def matrix(gathered, place):
        return gathered[:, place * rows : (place + 1) * rows].astype(BF16).reshape(width, width)

    def notes(gathered):
        return gathered[:, 2 * rows :, :rows].astype(F32).transpose(1, 0, 2).reshape(NOTE_ROWS, width)

    matrices = (matrix(mine, 0), matrix(theirs, 0), matrix(theirs, 1), matrix(mine, 1))
    new_trans, new_covariance, new_offset, new_counts = combine(
        step_counts, trans, covar, offset_vec, jnp.concatenate([notes(mine), notes(theirs)]), matrices
    )
    return (new_trans[None], new_covariance[None], new_offset, new_counts)


def solution(mesh):
    in_specs = (
        P("tm", "state", None),
        P("tm", "state", None),
        P("tm", "state", None),
        P("tm", "state"),
        P("tm", "state"),
        P("tm"),
        P(),
    )
    out_specs = (P("tm", "state", None), P("tm", "state", None), P("tm", "state"), P("tm"))
    return jax.shard_map(local, mesh=mesh, in_specs=in_specs, out_specs=out_specs, check_vma=False)
```
